32 devices in a mesh: state: 2 (over x), row: 4 (over y, core), col: 4 (over z).
Axes of the slice: x: 2, y: 2, z: 4, core: 2. Of those that a mesh axis runs over, the one named last changes fastest.
Arguments:
- coeff_rows: bfloat16 [2048, 4096], P('row', 'state'), may hold values from -0.09375 to 0.09375
- coeff_cols: bfloat16 [4096, 4096], P('col', 'state'), may hold values from -0.09375 to 0.09375
- occupation: float32 [4096], P('state'), may hold values from 0.05 to 2
- send_list: int32 [2, 4, 4, 4, 2], P('state', 'row', 'col'), may hold values from 0 to 4
- row_phi: bfloat16 [2, 4, 4, 8, 256, 256], P('state', 'row', 'col'), may hold values from -6 to 6
- col_phi: bfloat16 [2, 4, 4, 8, 256, 256], P('state', 'row', 'col'), may hold values from -6 to 6
Outputs:
- density: float32 [2, 4, 4, 256], P('state', 'row', 'col')
The draws below stay inside these ranges and needn't reach their ends.
Inputs may be any that keep to these rules, and one draw needn't show every extreme that they name: `send_list`: a value of 4 relays nothing.
All inputs are finite; a program needn't handle non-finite values.
Results may differ from the reference program's by a relative error of at most 0.004.
Values may be sent and summed in bfloat16 or wider, within the bound.
No kernel may reach another device: no remote copies, remote signals or barrier semaphores. Data moves between devices by JAX's collectives and lax.ppermute only.
A program may use at most 64 MiB of HBM per device.

```python
import math
import jax
import jax.numpy as jnp
from jax import lax

NS = 4096
PTS = 256
SLOTS = 2
NR = 2048
NC = 4096
SUB = 256
NSUB = 4
RECV = 8
N_STATE = 2
N_ROW = 4
N_COL = 4


def with_ends(entries, own_key, low, largest):
    dims = entries.shape
    spot = [jax.random.randint(jax.random.fold_in(own_key, axis), (), 0, dims[axis]) for axis in range(len(dims))]
    entries = entries.at[tuple(spot)].set(low)
    longest = dims.index(max(dims))
    spot[longest] = (spot[longest] + 1) % dims[longest]
    return entries.at[tuple(spot)].set(largest)


def block_levels(key, extent, pieces, low, largest):
    def one(dim, blocks):
        heights = jax.random.uniform(jax.random.fold_in(jax.random.fold_in(key, 6), dim), (blocks,), jnp.float32, low / len(pieces), largest / len(pieces))
        return jnp.repeat(jnp.exp(heights), extent[dim] // blocks).reshape((-1,) + (1,) * (len(extent) - dim - 1))

    level = one(*pieces[0])
    for cut in pieces[1:]:
        level = level * one(*cut)
    return level


def bell_draw(stream_key, extent, deviation, reach, pieces=(), kind=jnp.bfloat16):
    gain = block_levels(stream_key, extent, pieces, -0.22, 0.18) if pieces else 1.0
    entries = jax.random.normal(stream_key, extent, jnp.float32) * deviation * gain
    return jnp.minimum(jnp.maximum(entries, -reach), reach).astype(kind)


def setup_inputs(seed: int = 0) -> dict:
    key_of = jax.random.split(jax.random.key(seed), 7)
    return {
        "coeff_rows": bell_draw(key_of[0], (NR, NS), NS ** -0.5, 0.09375, ((0, 4), (1, 2))),
        "coeff_cols": bell_draw(key_of[1], (NC, NS), NS ** -0.5, 0.09375, ((0, 4), (1, 2))),
        "occupation": jnp.clip(jnp.exp(math.log(2.0) - 3.6888794 * jax.random.uniform(key_of[2], (NS,), jnp.float32) ** block_levels(key_of[2], (NS,), ((0, 2),), -0.2, 0.2)), 0.05, 2.0),
        "send_list": with_ends(jax.random.randint(key_of[3], (N_STATE, N_ROW, N_COL, N_ROW, SLOTS), 0, NSUB + 1), jax.random.fold_in(key_of[3], 1), 0, NSUB).astype(jnp.int32),
        "row_phi": bell_draw(key_of[4], (N_STATE, N_ROW, N_COL, RECV, SUB, PTS), 1.0, 6.0, ((0, 2), (1, 4), (2, 4))),
        "col_phi": bell_draw(key_of[5], (N_STATE, N_ROW, N_COL, RECV, SUB, PTS), 1.0, 6.0, ((0, 2), (1, 4), (2, 4))),
    }


def reference(coeff_rows, coeff_cols, occupation, send_list, row_phi, col_phi):
    weighted = (coeff_rows.astype(jnp.float32) * occupation[None, :]).astype(jnp.bfloat16)
    matrix = jnp.dot(weighted, coeff_cols.T, preferred_element_type=jnp.float32).astype(jnp.bfloat16)
    tiles = matrix.reshape(N_ROW, N_STATE, SUB, N_COL, NSUB, SUB).transpose(1, 0, 3, 4, 2, 5)
    blank = jnp.zeros((N_STATE, N_ROW, N_COL, 1, SUB, SUB), jnp.bfloat16)
    tiles = jnp.concatenate([tiles, blank], axis=3)
    sources = jnp.arange(N_ROW, dtype=jnp.int32)

    def owner(index):
        s_idx = index // (N_ROW * N_COL)
        r_idx = (index // N_COL) % N_ROW
        c_idx = index % N_COL
        chosen = tiles[s_idx, :, c_idx]
        picks = send_list[s_idx, :, c_idx, r_idx, :]
        got = chosen[sources[:, None], picks].reshape(RECV, SUB, SUB)
        half = jnp.einsum('tab,tbp->tap', got.astype(jnp.float32), col_phi[s_idx, r_idx, c_idx].astype(jnp.float32))
        return jnp.sum(row_phi[s_idx, r_idx, c_idx].astype(jnp.float32) * half, axis=(0, 1))

    owners = jnp.arange(N_STATE * N_ROW * N_COL, dtype=jnp.int32)
    return lax.map(owner, owners).reshape(N_STATE, N_ROW, N_COL, PTS)
```

```python
import functools

import jax
import jax.numpy as jnp
from jax import lax
from jax.experimental import pallas as pl
from jax.experimental.pallas import tpu as pltpu
from jax.sharding import PartitionSpec as P

CHUNKS = 2
VMEM_LIMIT = 24 * 1024 * 1024
NT = (((1,), (1,)), ((), ()))


def params():
    return pltpu.CompilerParams(vmem_limit_bytes=VMEM_LIMIT)


def product_kernel(block_ref, rows_ref, occ_ref, cols_ref, *refs):
    outs, weighted_ref = refs[:-1], refs[-1]

    @pl.when(pl.program_id(0) == 0)
    def _():
        weighted_ref[...] = (rows_ref[...].astype(jnp.float32) * occ_ref[...]).astype(jnp.bfloat16)

    total = lax.dot_general(weighted_ref[...], cols_ref[...], NT, preferred_element_type=jnp.float32)
    height = total.shape[0] // len(outs)
    for n, out in enumerate(outs):
        out[...] = total[n * height : (n + 1) * height].astype(out.dtype)


def product(block, coeff_rows, occupation, coeff_cols, side, pieces, dtype):
    states, width = coeff_rows.shape[1], coeff_cols.shape[0]
    step = min(256, width)
    height = side // pieces
    return pl.pallas_call(
        product_kernel,
        grid_spec=pltpu.PrefetchScalarGridSpec(
            num_scalar_prefetch=1,
            grid=(width // step,),
            in_specs=[
                pl.BlockSpec((side, states), lambda j, b: (b[0], 0)),
                pl.BlockSpec((1, states), lambda j, b: (0, 0)),
                pl.BlockSpec((step, states), lambda j, b: (j, 0)),
            ],
            out_specs=[pl.BlockSpec((height, step), lambda j, b: (0, j))] * pieces,
            scratch_shapes=[pltpu.VMEM((side, states), jnp.bfloat16)],
        ),
        out_shape=[jax.ShapeDtypeStruct((height, width), dtype)] * pieces,
        compiler_params=params(),
        cost_estimate=pl.CostEstimate(
            flops=2 * side * states * width, bytes_accessed=2 * states * (width + side), transcendentals=0
        ),
    )(block, coeff_rows, occupation, coeff_cols)


def pick_kernel(slots, picks_ref, own_ref, *refs):
    tiles_ref = refs[-1]
    owners = picks_ref.shape[0] // slots
    parts, outs = refs[: -1 - owners], refs[-1 - owners : -1]
    count, height, side = tiles_ref.shape[0] - 1, tiles_ref.shape[1], tiles_ref.shape[2]
    for t in range(count):
        cut = slice(t * side, (t + 1) * side)
        total = own_ref[:, cut]
        for part in parts:
            total = total + part[:, cut].astype(jnp.float32)
        tiles_ref[t] = total.astype(jnp.bfloat16)
    tiles_ref[count] = jnp.zeros((height, side), jnp.bfloat16)
    for d, out in enumerate(outs):
        for k in range(slots):
            out[k] = tiles_ref[picks_ref[d * slots + k]]


def pick(picks, own, parts, side, owners, slots):
    height, width = own.shape
    return pl.pallas_call(
        functools.partial(pick_kernel, slots),
        in_specs=[pl.BlockSpec(memory_space=pltpu.SMEM)]
        + [pl.BlockSpec(memory_space=pltpu.VMEM)] * (1 + len(parts)),
        out_specs=[pl.BlockSpec(memory_space=pltpu.VMEM)] * owners,
        out_shape=[jax.ShapeDtypeStruct((slots, height, side), jnp.bfloat16)] * owners,
        scratch_shapes=[pltpu.VMEM((width // side + 1, height, side), jnp.bfloat16)],
        compiler_params=params(),
        cost_estimate=pl.CostEstimate(flops=height * width, bytes_accessed=8 * height * width, transcendentals=0),
    )(picks, own, *parts)


def contract_kernel(sources_ref, before_ref, row_phi_ref, col_phi_ref, *refs):
    gots, out = refs[:-1], refs[-1]
    density = before_ref[...]
    for d, got in enumerate(gots):
        slots = got.shape[0]
        for k in range(slots):
            m = sources_ref[d] * slots + k
            half = jnp.dot(got[k], col_phi_ref[m], preferred_element_type=jnp.float32)
            density += jnp.sum(row_phi_ref[m].astype(jnp.float32) * half, axis=0, keepdims=True)
    out[...] = density


def contract(sources, before, row_phi, col_phi, gots, chunk):
    received, side, points = col_phi.shape
    slots, height, _ = gots[0].shape
    return pl.pallas_call(
        contract_kernel,
        grid=(1,),
        in_specs=[
            pl.BlockSpec(memory_space=pltpu.SMEM),
            pl.BlockSpec((1, points), lambda j: (0, 0)),
            pl.BlockSpec((received, height, points), lambda j: (0, chunk, 0)),
            pl.BlockSpec((received, side, points), lambda j: (0, 0, 0)),
        ]
        + [pl.BlockSpec((slots, height, side), lambda j: (0, 0, 0))] * len(gots),
        out_specs=pl.BlockSpec((1, points), lambda j: (0, 0)),
        out_shape=jax.ShapeDtypeStruct((1, points), jnp.float32),
        compiler_params=params(),
        cost_estimate=pl.CostEstimate(
            flops=2 * received * height * side * points, bytes_accessed=2 * received * side * points, transcendentals=0
        ),
    )(sources, before, row_phi, col_phi, *gots)


def swap(value, axis, d):
    return lax.ppermute(value, axis, [(i, i ^ d) for i in range(lax.axis_size(axis))])


def local(coeff_rows, coeff_cols, occupation, send_list, row_phi, col_phi):
    states, owners = lax.axis_size("state"), lax.axis_size("row")
    state, row = lax.axis_index("state"), lax.axis_index("row")
    side = coeff_rows.shape[0] // states
    slots = send_list.shape[-1]
    row_phi, col_phi = row_phi[0, 0, 0], col_phi[0, 0, 0]
    occupation = occupation[None, :]
    sources = jnp.bitwise_xor(row, jnp.arange(owners, dtype=jnp.int32))
    picks = send_list[0, 0, 0][sources].reshape(-1)

    arrived = [[] for _ in range(CHUNKS)]
    for d in range(1, states):
        target = jnp.bitwise_xor(state, d).astype(jnp.int32)[None]
        sent = product(target, coeff_rows, occupation, coeff_cols, side, CHUNKS, jnp.bfloat16)
        for c in range(CHUNKS):
            arrived[c].append(swap(sent[c], "state", d))
    own = product(state.astype(jnp.int32)[None], coeff_rows, occupation, coeff_cols, side, CHUNKS, jnp.float32)

    density = jnp.zeros((1, row_phi.shape[-1]), jnp.float32)
    for c in range(CHUNKS):
        outgoing = pick(picks, own[c], arrived[c], side, owners, slots)
        gots = [outgoing[0]] + [swap(outgoing[d], "row", d) for d in range(1, owners)]
        density = contract(sources, density, row_phi, col_phi, gots, c)
    return density.reshape(1, 1, 1, -1)


def solution(mesh):
    in_specs = (
        P("row", "state"),
        P("col", "state"),
        P("state"),
        P("state", "row", "col", None, None),
        P("state", "row", "col", None, None, None),
        P("state", "row", "col", None, None, None),
    )
    out_specs = P("state", "row", "col", None)
    return jax.shard_map(local, mesh=mesh, in_specs=in_specs, out_specs=out_specs, check_vma=False)
```

```python
import functools

import jax
import jax.numpy as jnp
from jax import lax
from jax.experimental import pallas as pl
from jax.experimental.pallas import tpu as pltpu
from jax.sharding import PartitionSpec as P

EIGHTHS = (3, 3, 2)
MIB = 1024 * 1024
NT = (((1,), (1,)), ((), ()))
VMEM = pl.BlockSpec(memory_space=pltpu.VMEM)
SMEM = pl.BlockSpec(memory_space=pltpu.SMEM)
HBM = pl.BlockSpec(memory_space=pltpu.HBM)


def params(mib):
    return pltpu.CompilerParams(vmem_limit_bytes=mib * MIB)


def first_kernel(rows_hbm, occ_hbm, cols_hbm, out, rows_ref, occ_ref, cols_ref, occ_sem, rows_sem, cols_sem):
    side, states = rows_ref.shape
    height = cols_ref.shape[1]
    block = pl.multiple_of((lax.axis_index("state") ^ 1) * side, side)
    copies = [
        pltpu.make_async_copy(occ_hbm, occ_ref, occ_sem),
        pltpu.make_async_copy(rows_hbm.at[pl.ds(block, side)], rows_ref, rows_sem),
        pltpu.make_async_copy(cols_hbm.at[:, pl.ds(0, height)], cols_ref, cols_sem),
    ]
    for copy in copies:
        copy.start()
    copies[0].wait()
    copies[1].wait()
    weighted = (rows_ref[...].astype(jnp.float32) * occ_ref[...]).astype(jnp.bfloat16)
    copies[2].wait()
    total = lax.dot_general(cols_ref[...].reshape(-1, states), weighted, NT, preferred_element_type=jnp.float32)
    out[...] = total.reshape(out.shape).astype(out.dtype)


def first(height, coeff_rows, occupation, coeff_cols, side):
    count, _, states = coeff_cols.shape
    operands = (coeff_rows, occupation, coeff_cols)
    return pl.pallas_call(
        first_kernel,
        in_specs=[HBM] * 3,
        out_specs=VMEM,
        out_shape=jax.ShapeDtypeStruct((count, height, side), jnp.bfloat16),
        scratch_shapes=[
            pltpu.VMEM((side, states), jnp.bfloat16),
            pltpu.VMEM((1, states), jnp.float32),
            pltpu.VMEM((count, height, states), jnp.bfloat16),
            pltpu.SemaphoreType.DMA,
            pltpu.SemaphoreType.DMA,
            pltpu.SemaphoreType.DMA,
        ],
        compiler_params=params(16),
        cost_estimate=pl.CostEstimate(
            flops=2 * side * states * count * height,
            bytes_accessed=2 * states * (count * height + side),
            transcendentals=0,
        ),
    )(*(pltpu.with_memory_space_constraint(x, pltpu.HBM) for x in operands))


def rest_kernel(heights, rows_ref, occ_ref, cols_ref, *refs):
    outs, weighted_ref = list(refs[:-1]), refs[-1]
    groups, side = weighted_ref.shape[0] // cols_ref.shape[1], cols_ref.shape[1]
    states = weighted_ref.shape[1]
    state = lax.axis_index("state")
    for d in range(groups):
        rows = rows_ref[pl.ds(pl.multiple_of((state ^ d) * side, side), side)]
        weighted_ref[d * side : (d + 1) * side] = (rows.astype(jnp.float32) * occ_ref[...]).astype(jnp.bfloat16)
    start = 0
    for c, height in enumerate(heights):
        cols = cols_ref[:, start : start + height].reshape(-1, states)
        total = lax.dot_general(cols, weighted_ref[...], NT, preferred_element_type=jnp.float32)
        for d in range(groups):
            if (c, d) != (0, 1):
                out = outs.pop(0)
                out[...] = total[:, d * side : (d + 1) * side].reshape(out.shape).astype(out.dtype)
        start += height


def rest(heights, coeff_rows, occupation, coeff_cols, side):
    count, _, states = coeff_cols.shape
    groups = coeff_rows.shape[0] // side
    keys = [(c, d) for c in range(len(heights)) for d in range(groups) if (c, d) != (0, 1)]
    outs = pl.pallas_call(
        functools.partial(rest_kernel, heights),
        in_specs=[VMEM] * 3,
        out_specs=[VMEM] * len(keys),
        out_shape=[
            jax.ShapeDtypeStruct((count, heights[c], side), jnp.bfloat16 if d else jnp.float32) for c, d in keys
        ],
        scratch_shapes=[pltpu.VMEM((groups * side, states), jnp.bfloat16)],
        compiler_params=params(16),
        cost_estimate=pl.CostEstimate(
            flops=2 * groups * side * states * count * side,
            bytes_accessed=2 * states * (count + groups) * side,
            transcendentals=0,
        ),
    )(coeff_rows, occupation, coeff_cols)
    return dict(zip(keys, outs))


def pick_kernel(picks_ref, own_ref, *refs):
    tiles_ref = refs[-1]
    owners, slots = picks_ref.shape
    row = lax.axis_index("row")
    parts, outs = refs[: -1 - owners], refs[-1 - owners : -1]
    count = own_ref.shape[0]
    total = own_ref[...]
    for part in parts:
        total = total + part[...].astype(jnp.float32)
    tiles_ref[:count] = total.astype(jnp.bfloat16)
    tiles_ref[count] = jnp.zeros(tiles_ref.shape[1:], jnp.bfloat16)
    for d, out in enumerate(outs):
        for k in range(slots):
            out[k] = tiles_ref[picks_ref[row ^ d, k]]


def pick(picks, own, parts):
    count, height, side = own.shape
    owners, slots = picks.shape
    return pl.pallas_call(
        pick_kernel,
        in_specs=[SMEM] + [VMEM] * (1 + len(parts)),
        out_specs=[VMEM] * owners,
        out_shape=[jax.ShapeDtypeStruct((slots, height, side), jnp.bfloat16)] * owners,
        scratch_shapes=[pltpu.VMEM((count + 1, height, side), jnp.bfloat16)],
        compiler_params=params(8),
        cost_estimate=pl.CostEstimate(
            flops=count * height * side, bytes_accessed=8 * count * height * side, transcendentals=0
        ),
    )(picks, own, *parts)


def contract_kernel(start, before_ref, row_phi_ref, col_phi_ref, *refs):
    gots, out = refs[:-1], refs[-1]
    row = lax.axis_index("row")
    cut = pl.ds(start, gots[0].shape[1])
    density = before_ref[...]
    for d, got in enumerate(gots):
        slots = got.shape[0]
        for k in range(slots):
            m = (row ^ d) * slots + k
            half = jnp.dot(got[k], row_phi_ref[m], preferred_element_type=jnp.float32)
            density += jnp.sum(col_phi_ref[m, cut].astype(jnp.float32) * half, axis=0, keepdims=True)
    out[...] = density


def contract(before, row_phi, col_phi, gots, start):
    received, side, points = col_phi.shape
    height = gots[0].shape[1]
    return pl.pallas_call(
        functools.partial(contract_kernel, start),
        in_specs=[VMEM] * (3 + len(gots)),
        out_specs=VMEM,
        out_shape=jax.ShapeDtypeStruct((1, points), jnp.float32),
        compiler_params=params(8),
        cost_estimate=pl.CostEstimate(
            flops=2 * received * height * side * points, bytes_accessed=2 * received * side * points, transcendentals=0
        ),
    )(before, row_phi, col_phi, *gots)


def swap(value, axis, d):
    return lax.ppermute(value, axis, [(i, i ^ d) for i in range(lax.axis_size(axis))])


def local(coeff_rows, coeff_cols, occupation, send_list, row_phi, col_phi):
    states, owners = lax.axis_size("state"), lax.axis_size("row")
    side = coeff_rows.shape[0] // states
    heights = [side * n // 8 for n in EIGHTHS]
    row_phi, col_phi, picks = row_phi[0, 0, 0], col_phi[0, 0, 0], send_list[0, 0, 0]
    factors = coeff_rows, occupation[None, :], coeff_cols.reshape(-1, side, coeff_cols.shape[1]), side

    early = first(heights[0], *factors)
    parts = rest(heights, *factors)
    parts[0, 1] = early
    arrived = [[swap(parts[c, d], "state", d) for d in range(1, states)] for c in range(len(heights))]

    density = jnp.zeros((1, row_phi.shape[-1]), jnp.float32)
    for c in range(len(heights)):
        outgoing = pick(picks, parts[c, 0], arrived[c])
        gots = [outgoing[0]] + [swap(outgoing[d], "row", d) for d in range(1, owners)]
        density = contract(density, row_phi, col_phi, gots, sum(heights[:c]))
    return density.reshape(1, 1, 1, -1)


def solution(mesh):
    in_specs = (
        P("row", "state"),
        P("col", "state"),
        P("state"),
        P("state", "row", "col", None, None),
        P("state", "row", "col", None, None, None),
        P("state", "row", "col", None, None, None),
    )
    out_specs = P("state", "row", "col", None)
    return jax.shard_map(local, mesh=mesh, in_specs=in_specs, out_specs=out_specs, check_vma=False)
```

```python
import functools

import jax
import jax.numpy as jnp
from jax import lax
from jax.experimental import pallas as pl
from jax.experimental.pallas import tpu as pltpu
from jax.sharding import PartitionSpec as P

EIGHTHS = (3, 3, 2)
MIB = 1024 * 1024
NT = (((1,), (1,)), ((), ()))
VMEM = pl.BlockSpec(memory_space=pltpu.VMEM)
SMEM = pl.BlockSpec(memory_space=pltpu.SMEM)
HBM = pl.BlockSpec(memory_space=pltpu.HBM)
ANY = pl.BlockSpec(memory_space=pl.ANY)
NEAR = 2
STEP_FLOPS = 3 * 10**9


def params(mib):
    return pltpu.CompilerParams(vmem_limit_bytes=mib * MIB)


def first_kernel(rows_hbm, occ_hbm, cols_hbm, out, rows_ref, occ_ref, cols_ref, occ_sem, rows_sem, cols_sem):
    side, states = rows_ref.shape
    height = cols_ref.shape[1]
    block = pl.multiple_of((lax.axis_index("state") ^ 1) * side, side)
    copies = [
        pltpu.make_async_copy(occ_hbm, occ_ref, occ_sem),
        pltpu.make_async_copy(rows_hbm.at[pl.ds(block, side)], rows_ref, rows_sem),
        pltpu.make_async_copy(cols_hbm.at[:, pl.ds(0, height)], cols_ref, cols_sem),
    ]
    for copy in copies:
        copy.start()
    copies[0].wait()
    copies[1].wait()
    weighted = (rows_ref[...].astype(jnp.float32) * occ_ref[...]).astype(jnp.bfloat16)
    copies[2].wait()
    total = lax.dot_general(cols_ref[...].reshape(-1, states), weighted, NT, preferred_element_type=jnp.float32)
    out[...] = total.reshape(out.shape).astype(out.dtype)


def first(height, coeff_rows, occupation, coeff_cols, side):
    count, _, states = coeff_cols.shape
    operands = (coeff_rows, occupation, coeff_cols)
    return pl.pallas_call(
        first_kernel,
        in_specs=[HBM] * 3,
        out_specs=VMEM,
        out_shape=jax.ShapeDtypeStruct((count, height, side), jnp.bfloat16),
        scratch_shapes=[
            pltpu.VMEM((side, states), jnp.bfloat16),
            pltpu.VMEM((1, states), jnp.float32),
            pltpu.VMEM((count, height, states), jnp.bfloat16),
            pltpu.SemaphoreType.DMA,
            pltpu.SemaphoreType.DMA,
            pltpu.SemaphoreType.DMA,
        ],
        compiler_params=params(16),
        cost_estimate=pl.CostEstimate(
            flops=2 * side * states * count * height,
            bytes_accessed=2 * states * (count * height + side),
            transcendentals=0,
        ),
    )(*(pltpu.with_memory_space_constraint(x, pltpu.HBM) for x in operands))


def rest_kernel(heights, rows_ref, occ_ref, cols_ref, _, *refs):
    outs, weighted_ref = list(refs[:-1]), refs[-1]
    groups, side = weighted_ref.shape[0] // cols_ref.shape[1], cols_ref.shape[1]
    states = weighted_ref.shape[1]
    state = lax.axis_index("state")
    for d in range(groups):
        rows = rows_ref[pl.ds(pl.multiple_of((state ^ d) * side, side), side)]
        weighted_ref[d * side : (d + 1) * side] = (rows.astype(jnp.float32) * occ_ref[...]).astype(jnp.bfloat16)
    start = 0
    for c, height in enumerate(heights):
        cols = cols_ref[:, start : start + height].reshape(-1, states)
        total = lax.dot_general(cols, weighted_ref[...], NT, preferred_element_type=jnp.float32)
        for d in range(groups):
            if (c, d) != (0, 1):
                out = outs.pop(0)
                out[...] = total[:, d * side : (d + 1) * side].reshape(out.shape).astype(out.dtype)
        start += height


def rest(heights, coeff_rows, occupation, coeff_cols, side, after):
    count, _, states = coeff_cols.shape
    groups = coeff_rows.shape[0] // side
    keys = [(c, d) for c in range(len(heights)) for d in range(groups) if (c, d) != (0, 1)]
    outs = pl.pallas_call(
        functools.partial(rest_kernel, heights),
        in_specs=[VMEM] * 3 + [ANY],
        out_specs=[VMEM] * len(keys),
        out_shape=[
            jax.ShapeDtypeStruct((count, heights[c], side), jnp.bfloat16 if d else jnp.float32) for c, d in keys
        ],
        scratch_shapes=[pltpu.VMEM((groups * side, states), jnp.bfloat16)],
        compiler_params=params(16),
        cost_estimate=pl.CostEstimate(
            flops=2 * groups * side * states * count * side,
            bytes_accessed=2 * states * (count + groups) * side,
            transcendentals=0,
        ),
    )(coeff_rows, occupation, coeff_cols, after)
    return dict(zip(keys, outs))


def spread_kernel(picks_ref, out):
    owners, slots = picks_ref.shape
    row = lax.axis_index("row")
    for d in range(owners):
        for k in range(slots):
            out[d * slots + k] = jnp.full(out.shape[1:], picks_ref[row ^ d, k], jnp.int32)


def spread(picks, side):
    return pl.pallas_call(
        spread_kernel,
        in_specs=[SMEM],
        out_specs=VMEM,
        out_shape=jax.ShapeDtypeStruct((picks.size, 8, side), jnp.int32),
        compiler_params=params(8),
    )(picks)


def listed_tile(listed, tiles):
    chosen = jnp.zeros_like(tiles[0])
    for t, tile in enumerate(tiles):
        chosen = jnp.where(listed == t, tile, chosen)
    return chosen.astype(jnp.bfloat16)


def pick_kernel(groups, far, slots, lists_ref, own_ref, *refs):
    parts, tiles_ref, outs = refs[: groups - 1], refs[-1 - far], refs[-far:]
    tiles = []
    for t in range(own_ref.shape[0]):
        total = own_ref[t]
        for part in parts:
            total = total + part[t].astype(jnp.float32)
        tiles.append(total)
        tiles_ref[t] = total.astype(jnp.bfloat16)
    for d, out in enumerate(outs, NEAR):
        for k in range(slots):
            out[k] = listed_tile(lists_ref[d * slots + k, :1], tiles)


def pick(lists, slots, own, parts, after):
    count, height, side = own.shape
    owners = lists.shape[0] // slots
    return pl.pallas_call(
        functools.partial(pick_kernel, 1 + len(parts), owners - NEAR, slots),
        in_specs=[VMEM] * (2 + len(parts)) + [ANY] * len(after),
        out_specs=[VMEM] * (1 + owners - NEAR),
        out_shape=[jax.ShapeDtypeStruct((count, height, side), jnp.bfloat16)]
        + [jax.ShapeDtypeStruct((slots, height, side), jnp.bfloat16)] * (owners - NEAR),
        compiler_params=params(8),
        cost_estimate=pl.CostEstimate(
            flops=STEP_FLOPS, bytes_accessed=count * height * side, transcendentals=0
        ),
    )(lists, own, *parts, *after)


def near_kernel(slots, lists_ref, *refs):
    chunks, outs = refs[:-NEAR], refs[-NEAR:]
    start = 0
    for chunk in chunks:
        count, height, side = chunk.shape
        tiles = [chunk[t].astype(jnp.float32) for t in range(count)]
        for d, out in enumerate(outs):
            for k in range(slots):
                out[k, start : start + height] = listed_tile(lists_ref[d * slots + k, :1], tiles)
        start += height


def pick_near(lists, slots, chunks):
    side = sum(chunk.shape[1] for chunk in chunks)
    shape = jax.ShapeDtypeStruct((slots, side, chunks[0].shape[2]), jnp.bfloat16)
    return pl.pallas_call(
        functools.partial(near_kernel, slots),
        in_specs=[VMEM] * (1 + len(chunks)),
        out_specs=[VMEM] * NEAR,
        out_shape=[shape] * NEAR,
        compiler_params=params(8),
        cost_estimate=pl.CostEstimate(flops=STEP_FLOPS, bytes_accessed=side * side, transcendentals=0),
    )(lists, *chunks)


def contract_kernel(base, count, start, before_ref, row_phi_ref, col_phi_ref, *refs):
    gots, out = refs[:count], refs[-1]
    row = lax.axis_index("row")
    cut = pl.ds(start, gots[0].shape[1])
    density = before_ref[...]
    for d, got in enumerate(gots, base):
        slots = got.shape[0]
        for k in range(slots):
            m = (row ^ d) * slots + k
            half = jnp.dot(got[k], row_phi_ref[m], preferred_element_type=jnp.float32)
            density += jnp.sum(col_phi_ref[m, cut].astype(jnp.float32) * half, axis=0, keepdims=True)
    out[...] = density


def contract(before, row_phi, col_phi, gots, base, start, after=()):
    received, side, points = col_phi.shape
    slots, height, _ = gots[0].shape
    return pl.pallas_call(
        functools.partial(contract_kernel, base, len(gots), start),
        in_specs=[VMEM] * (3 + len(gots)) + [ANY] * len(after),
        out_specs=VMEM,
        out_shape=jax.ShapeDtypeStruct((1, points), jnp.float32),
        compiler_params=params(8),
        cost_estimate=pl.CostEstimate(
            flops=STEP_FLOPS,
            bytes_accessed=received * side * points,
            transcendentals=0,
        ),
    )(before, row_phi, col_phi, *gots, *after)


def swap(value, axis, d):
    return lax.ppermute(value, axis, [(i, i ^ d) for i in range(lax.axis_size(axis))])


def local(coeff_rows, coeff_cols, occupation, send_list, row_phi, col_phi):
    states, owners = lax.axis_size("state"), lax.axis_size("row")
    side, slots = coeff_rows.shape[0] // states, send_list.shape[-1]
    heights = [side * n // 8 for n in EIGHTHS]
    row_phi, col_phi, picks = row_phi[0, 0, 0], col_phi[0, 0, 0], send_list[0, 0, 0]
    factors = coeff_rows, occupation[None, :], coeff_cols.reshape(-1, side, coeff_cols.shape[1]), side

    lists = spread(picks, side)
    early = first(heights[0], *factors)
    parts = rest(heights, *factors, early)
    parts[0, 1] = early

    arrived = [[swap(parts[c, d], "state", d) for d in range(1, states)] for c in range(len(heights))]

    starts = [sum(heights[:c]) for c in range(len(heights))]
    tiles, far, after = [], [], []
    density = jnp.zeros((1, row_phi.shape[-1]), jnp.float32)
    for c in range(len(heights)):
        chunk, *outgoing = pick(lists, slots, parts[c, 0], arrived[c], after)
        tiles.append(chunk)
        after = [chunk]
        far.append([swap(out, "row", d) for d, out in enumerate(outgoing, NEAR)])
        if 1 <= c < len(heights) - 1:
            density = contract(density, row_phi, col_phi, far[c - 1], NEAR, starts[c - 1], after)
            after = [density]
    mine, other = pick_near(lists, slots, tiles)
    density = contract(density, row_phi, col_phi, far[-2], NEAR, starts[-2], [mine])
    density = contract(density, row_phi, col_phi, [mine, swap(other, "row", 1)], 0, 0)
    density = contract(density, row_phi, col_phi, far[-1], NEAR, starts[-1])
    return density.reshape(1, 1, 1, -1)


def solution(mesh):
    in_specs = (
        P("row", "state"),
        P("col", "state"),
        P("state"),
        P("state", "row", "col", None, None),
        P("state", "row", "col", None, None, None),
        P("state", "row", "col", None, None, None),
    )
    out_specs = P("state", "row", "col", None)
    return jax.shard_map(local, mesh=mesh, in_specs=in_specs, out_specs=out_specs, check_vma=False)
```

```python
import functools

import jax
import jax.numpy as jnp
from jax import lax
from jax.experimental import pallas as pl
from jax.experimental.pallas import tpu as pltpu
from jax.sharding import PartitionSpec as P

PARTS = (5, 7, 4)
MIB = 1024 * 1024
NT = (((1,), (1,)), ((), ()))
VMEM = pl.BlockSpec(memory_space=pltpu.VMEM)
SMEM = pl.BlockSpec(memory_space=pltpu.SMEM)
HBM = pl.BlockSpec(memory_space=pltpu.HBM)
ANY = pl.BlockSpec(memory_space=pl.ANY)
NEAR = 2
AHEAD = 2
STEP_FLOPS = 3 * 10**9


def params(mib):
    return pltpu.CompilerParams(vmem_limit_bytes=mib * MIB)


def first_kernel(rows_hbm, occ_hbm, cols_hbm, out, rows_ref, occ_ref, cols_ref, occ_sem, rows_sem, cols_sem):
    side, states = rows_ref.shape
    height = cols_ref.shape[1]
    block = pl.multiple_of((lax.axis_index("state") ^ 1) * side, side)
    copies = [
        pltpu.make_async_copy(occ_hbm, occ_ref, occ_sem),
        pltpu.make_async_copy(rows_hbm.at[pl.ds(block, side)], rows_ref, rows_sem),
        pltpu.make_async_copy(cols_hbm.at[:, pl.ds(0, height)], cols_ref, cols_sem),
    ]
    for copy in copies:
        copy.start()
    copies[0].wait()
    copies[1].wait()
    weighted = (rows_ref[...].astype(jnp.float32) * occ_ref[...]).astype(jnp.bfloat16)
    copies[2].wait()
    total = lax.dot_general(cols_ref[...].reshape(-1, states), weighted, NT, preferred_element_type=jnp.float32)
    out[...] = total.reshape(out.shape).astype(out.dtype)


def first(height, coeff_rows, occupation, coeff_cols, side):
    count, _, states = coeff_cols.shape
    operands = (coeff_rows, occupation, coeff_cols)
    return pl.pallas_call(
        first_kernel,
        in_specs=[HBM] * 3,
        out_specs=VMEM,
        out_shape=jax.ShapeDtypeStruct((count, height, side), jnp.bfloat16),
        scratch_shapes=[
            pltpu.VMEM((side, states), jnp.bfloat16),
            pltpu.VMEM((1, states), jnp.float32),
            pltpu.VMEM((count, height, states), jnp.bfloat16),
            pltpu.SemaphoreType.DMA,
            pltpu.SemaphoreType.DMA,
            pltpu.SemaphoreType.DMA,
        ],
        compiler_params=params(16),
        cost_estimate=pl.CostEstimate(
            flops=2 * side * states * count * height,
            bytes_accessed=2 * states * (count * height + side),
            transcendentals=0,
        ),
    )(*(pltpu.with_memory_space_constraint(x, pltpu.HBM) for x in operands))


def rest_kernel(heights, rows_ref, occ_ref, cols_ref, _, *refs):
    outs, weighted_ref = list(refs[:-1]), refs[-1]
    groups, side = weighted_ref.shape[0] // cols_ref.shape[1], cols_ref.shape[1]
    states = weighted_ref.shape[1]
    state = lax.axis_index("state")
    for d in range(groups):
        rows = rows_ref[pl.ds(pl.multiple_of((state ^ d) * side, side), side)]
        weighted_ref[d * side : (d + 1) * side] = (rows.astype(jnp.float32) * occ_ref[...]).astype(jnp.bfloat16)
    start = 0
    for c, height in enumerate(heights):
        cols = cols_ref[:, start : start + height].reshape(-1, states)
        total = lax.dot_general(cols, weighted_ref[...], NT, preferred_element_type=jnp.float32)
        for d in range(groups):
            if (c, d) != (0, 1):
                out = outs.pop(0)
                out[...] = total[:, d * side : (d + 1) * side].reshape(out.shape).astype(out.dtype)
        start += height


def rest(heights, coeff_rows, occupation, coeff_cols, side, after):
    count, _, states = coeff_cols.shape
    groups = coeff_rows.shape[0] // side
    keys = [(c, d) for c in range(len(heights)) for d in range(groups) if (c, d) != (0, 1)]
    outs = pl.pallas_call(
        functools.partial(rest_kernel, heights),
        in_specs=[VMEM] * 3 + [ANY],
        out_specs=[VMEM] * len(keys),
        out_shape=[
            jax.ShapeDtypeStruct((count, heights[c], side), jnp.bfloat16 if d else jnp.float32) for c, d in keys
        ],
        scratch_shapes=[pltpu.VMEM((groups * side, states), jnp.bfloat16)],
        compiler_params=params(16),
        cost_estimate=pl.CostEstimate(
            flops=2 * groups * side * states * count * side,
            bytes_accessed=2 * states * (count + groups) * side,
            transcendentals=0,
        ),
    )(coeff_rows, occupation, coeff_cols, after)
    return dict(zip(keys, outs))


def spread_kernel(picks_ref, out):
    owners, slots = picks_ref.shape
    row = lax.axis_index("row")
    for d in range(owners):
        for k in range(slots):
            out[d * slots + k] = jnp.full(out.shape[1:], picks_ref[row ^ d, k], jnp.int32)


def spread(picks, side):
    return pl.pallas_call(
        spread_kernel,
        in_specs=[SMEM],
        out_specs=VMEM,
        out_shape=jax.ShapeDtypeStruct((picks.size, 8, side), jnp.int32),
        compiler_params=params(8),
    )(picks)


def listed_tile(listed, tiles):
    chosen = jnp.zeros_like(tiles[0])
    for t, tile in enumerate(tiles):
        chosen = jnp.where(listed == t, tile, chosen)
    return chosen.astype(jnp.bfloat16)


def pick_kernel(groups, far, slots, lists_ref, own_ref, *refs):
    parts, tiles_ref, outs = refs[: groups - 1], refs[-1 - far], refs[-far:]
    tiles = []
    for t in range(own_ref.shape[0]):
        total = own_ref[t]
        for part in parts:
            total = total + part[t].astype(jnp.float32)
        tiles.append(total)
        tiles_ref[t] = total.astype(jnp.bfloat16)
    for d, out in enumerate(outs, NEAR):
        for k in range(slots):
            out[k] = listed_tile(lists_ref[d * slots + k, :1], tiles)


def pick(lists, slots, own, parts, after):
    count, height, side = own.shape
    owners = lists.shape[0] // slots
    return pl.pallas_call(
        functools.partial(pick_kernel, 1 + len(parts), owners - NEAR, slots),
        in_specs=[VMEM] * (2 + len(parts)) + [ANY] * len(after),
        out_specs=[VMEM] * (1 + owners - NEAR),
        out_shape=[jax.ShapeDtypeStruct((count, height, side), jnp.bfloat16)]
        + [jax.ShapeDtypeStruct((slots, height, side), jnp.bfloat16)] * (owners - NEAR),
        compiler_params=params(8),
        cost_estimate=pl.CostEstimate(
            flops=STEP_FLOPS, bytes_accessed=count * height * side, transcendentals=0
        ),
    )(lists, own, *parts, *after)


def near_kernel(slots, lists_ref, *refs):
    chunks, outs = refs[:-NEAR], refs[-NEAR:]
    start = 0
    for chunk in chunks:
        count, height, side = chunk.shape
        tiles = [chunk[t].astype(jnp.float32) for t in range(count)]
        for d, out in enumerate(outs):
            for k in range(slots):
                out[k, start : start + height] = listed_tile(lists_ref[d * slots + k, :1], tiles)
        start += height


def pick_near(lists, slots, chunks):
    side = sum(chunk.shape[1] for chunk in chunks)
    shape = jax.ShapeDtypeStruct((slots, side, chunks[0].shape[2]), jnp.bfloat16)
    return pl.pallas_call(
        functools.partial(near_kernel, slots),
        in_specs=[VMEM] * (1 + len(chunks)),
        out_specs=[VMEM] * NEAR,
        out_shape=[shape] * NEAR,
        compiler_params=params(8),
        cost_estimate=pl.CostEstimate(flops=STEP_FLOPS, bytes_accessed=side * side, transcendentals=0),
    )(lists, *chunks)


def contract_kernel(base, count, start, before_ref, row_phi_ref, col_phi_ref, *refs):
    gots, out = refs[:count], refs[-1]
    row = lax.axis_index("row")
    cut = pl.ds(start, gots[0].shape[1])
    density = before_ref[...]
    for d, got in enumerate(gots, base):
        slots = got.shape[0]
        for k in range(slots):
            m = (row ^ d) * slots + k
            half = jnp.dot(got[k], row_phi_ref[m], preferred_element_type=jnp.float32)
            density += jnp.sum(col_phi_ref[m, cut].astype(jnp.float32) * half, axis=0, keepdims=True)
    out[...] = density


def contract(before, row_phi, col_phi, gots, base, start, after=()):
    received, side, points = col_phi.shape
    slots, height, _ = gots[0].shape
    return pl.pallas_call(
        functools.partial(contract_kernel, base, len(gots), start),
        in_specs=[VMEM] * (3 + len(gots)) + [ANY] * len(after),
        out_specs=VMEM,
        out_shape=jax.ShapeDtypeStruct((1, points), jnp.float32),
        compiler_params=params(8),
        cost_estimate=pl.CostEstimate(
            flops=STEP_FLOPS,
            bytes_accessed=received * side * points,
            transcendentals=0,
        ),
    )(before, row_phi, col_phi, *gots, *after)


def swap(value, axis, d):
    return lax.ppermute(value, axis, [(i, i ^ d) for i in range(lax.axis_size(axis))])


def local(coeff_rows, coeff_cols, occupation, send_list, row_phi, col_phi):
    states, owners = lax.axis_size("state"), lax.axis_size("row")
    side, slots = coeff_rows.shape[0] // states, send_list.shape[-1]
    bounds = [side * sum(PARTS[:n]) // sum(PARTS) // 16 * 16 for n in range(len(PARTS) + 1)]
    heights = [after - before for before, after in zip(bounds, bounds[1:])]
    row_phi, col_phi, picks = row_phi[0, 0, 0], col_phi[0, 0, 0], send_list[0, 0, 0]
    factors = coeff_rows, occupation[None, :], coeff_cols.reshape(-1, side, coeff_cols.shape[1]), side

    lists = spread(picks, side)
    early = first(heights[0], *factors)
    parts = rest(heights, *factors, early)
    parts[0, 1] = early

    def send(c):
        return [swap(parts[c, d], "state", d) for d in range(1, states)]

    arrived = [send(c) for c in range(min(AHEAD, len(heights)))]
    starts = [sum(heights[:c]) for c in range(len(heights))]
    tiles, far, after = [], [], []
    density = jnp.zeros((1, row_phi.shape[-1]), jnp.float32)
    for c in range(len(heights)):
        chunk, *outgoing = pick(lists, slots, parts[c, 0], arrived[c], after)
        tiles.append(chunk)
        after = [chunk]
        far.append([swap(out, "row", d) for d, out in enumerate(outgoing, NEAR)])
        if c + AHEAD < len(heights):
            for d in range(1, states):
                parts[c + AHEAD, d], _ = lax.optimization_barrier((parts[c + AHEAD, d], chunk))
            arrived.append(send(c + AHEAD))
        if 1 <= c < len(heights) - 1:
            density = contract(density, row_phi, col_phi, far[c - 1], NEAR, starts[c - 1], after)
            after = [density]
    mine, other = pick_near(lists, slots, tiles)
    density = contract(density, row_phi, col_phi, far[-2], NEAR, starts[-2], [mine])
    density = contract(density, row_phi, col_phi, [mine, swap(other, "row", 1)], 0, 0)
    density = contract(density, row_phi, col_phi, far[-1], NEAR, starts[-1])
    return density.reshape(1, 1, 1, -1)


def solution(mesh):
    in_specs = (
        P("row", "state"),
        P("col", "state"),
        P("state"),
        P("state", "row", "col", None, None),
        P("state", "row", "col", None, None, None),
        P("state", "row", "col", None, None, None),
    )
    out_specs = P("state", "row", "col", None)
    return jax.shard_map(local, mesh=mesh, in_specs=in_specs, out_specs=out_specs, check_vma=False)
```

```python
import functools

import jax
import jax.numpy as jnp
from jax import lax
from jax.experimental import pallas as pl
from jax.experimental.pallas import tpu as pltpu
from jax.sharding import PartitionSpec as P

PARTS = (5, 7, 4)
MIB = 1024 * 1024
NT = (((1,), (1,)), ((), ()))
VMEM = pl.BlockSpec(memory_space=pltpu.VMEM)
HBM = pl.BlockSpec(memory_space=pltpu.HBM)
ANY = pl.BlockSpec(memory_space=pl.ANY)
NEAR = 2
AHEAD = 2
STEP_FLOPS = 3 * 10**9


def params(mib):
    return pltpu.CompilerParams(vmem_limit_bytes=mib * MIB)


def first_kernel(rows_hbm, occ_hbm, cols_hbm, out, rows_ref, occ_ref, cols_ref, occ_sem, rows_sem, cols_sem):
    side, states = rows_ref.shape
    height = cols_ref.shape[1]
    block = pl.multiple_of((lax.axis_index("state") ^ 1) * side, side)
    copies = [
        pltpu.make_async_copy(occ_hbm, occ_ref, occ_sem),
        pltpu.make_async_copy(rows_hbm.at[pl.ds(block, side)], rows_ref, rows_sem),
        pltpu.make_async_copy(cols_hbm.at[:, pl.ds(0, height)], cols_ref, cols_sem),
    ]
    for copy in copies:
        copy.start()
    copies[0].wait()
    copies[1].wait()
    weighted = (rows_ref[...].astype(jnp.float32) * occ_ref[...]).astype(jnp.bfloat16)
    copies[2].wait()
    total = lax.dot_general(cols_ref[...].reshape(-1, states), weighted, NT, preferred_element_type=jnp.float32)
    out[...] = total.reshape(out.shape).astype(out.dtype)


def first(height, coeff_rows, occupation, coeff_cols, side):
    count, _, states = coeff_cols.shape
    operands = (coeff_rows, occupation, coeff_cols)
    return pl.pallas_call(
        first_kernel,
        in_specs=[HBM] * 3,
        out_specs=VMEM,
        out_shape=jax.ShapeDtypeStruct((count, height, side), jnp.bfloat16),
        scratch_shapes=[
            pltpu.VMEM((side, states), jnp.bfloat16),
            pltpu.VMEM((1, states), jnp.float32),
            pltpu.VMEM((count, height, states), jnp.bfloat16),
            pltpu.SemaphoreType.DMA,
            pltpu.SemaphoreType.DMA,
            pltpu.SemaphoreType.DMA,
        ],
        compiler_params=params(16),
        cost_estimate=pl.CostEstimate(
            flops=2 * side * states * count * height,
            bytes_accessed=2 * states * (count * height + side),
            transcendentals=0,
        ),
    )(*(pltpu.with_memory_space_constraint(x, pltpu.HBM) for x in operands))


def rest_kernel(heights, rows_ref, occ_ref, cols_ref, _, *refs):
    outs, weighted_ref = list(refs[:-1]), refs[-1]
    groups, side = weighted_ref.shape[0] // cols_ref.shape[1], cols_ref.shape[1]
    states = weighted_ref.shape[1]
    state = lax.axis_index("state")
    for d in range(groups):
        rows = rows_ref[pl.ds(pl.multiple_of((state ^ d) * side, side), side)]
        weighted_ref[d * side : (d + 1) * side] = (rows.astype(jnp.float32) * occ_ref[...]).astype(jnp.bfloat16)
    start = 0
    for c, height in enumerate(heights):
        cols = cols_ref[:, start : start + height].reshape(-1, states)
        total = lax.dot_general(cols, weighted_ref[...], NT, preferred_element_type=jnp.float32)
        for d in range(groups):
            if (c, d) != (0, 1):
                out = outs.pop(0)
                out[...] = total[:, d * side : (d + 1) * side].reshape(out.shape).astype(out.dtype)
        start += height


def rest(heights, coeff_rows, occupation, coeff_cols, side, after):
    count, _, states = coeff_cols.shape
    groups = coeff_rows.shape[0] // side
    keys = [(c, d) for c in range(len(heights)) for d in range(groups) if (c, d) != (0, 1)]
    outs = pl.pallas_call(
        functools.partial(rest_kernel, heights),
        in_specs=[VMEM] * 3 + [ANY],
        out_specs=[VMEM] * len(keys),
        out_shape=[
            jax.ShapeDtypeStruct((count, heights[c], side), jnp.bfloat16 if d else jnp.float32) for c, d in keys
        ],
        scratch_shapes=[pltpu.VMEM((groups * side, states), jnp.bfloat16)],
        compiler_params=params(16),
        cost_estimate=pl.CostEstimate(
            flops=2 * groups * side * states * count * side,
            bytes_accessed=2 * states * (count + groups) * side,
            transcendentals=0,
        ),
    )(coeff_rows, occupation, coeff_cols, after)
    return dict(zip(keys, outs))


def listed_tile(listed, tiles):
    chosen = jnp.zeros_like(tiles[0])
    for t, tile in enumerate(tiles):
        chosen = jnp.where(listed == t, tile, chosen)
    return chosen.astype(jnp.bfloat16)


def pick_kernel(groups, far, slots, lists_ref, own_ref, *refs):
    parts, tiles_ref, outs = refs[: groups - 1], refs[-1 - far], refs[-far:]
    row = lax.axis_index("row")
    tiles = []
    for t in range(own_ref.shape[0]):
        total = own_ref[t]
        for part in parts:
            total = total + part[t].astype(jnp.float32)
        tiles.append(total)
        tiles_ref[t] = total.astype(jnp.bfloat16)
    for d, out in enumerate(outs, NEAR):
        for k in range(slots):
            out[k] = listed_tile(lists_ref[(row ^ d) * slots + k, :1], tiles)


def pick(lists, slots, own, parts, after):
    count, height, side = own.shape
    owners = lists.shape[0] // slots
    return pl.pallas_call(
        functools.partial(pick_kernel, 1 + len(parts), owners - NEAR, slots),
        in_specs=[VMEM] * (2 + len(parts)) + [ANY] * len(after),
        out_specs=[VMEM] * (1 + owners - NEAR),
        out_shape=[jax.ShapeDtypeStruct((count, height, side), jnp.bfloat16)]
        + [jax.ShapeDtypeStruct((slots, height, side), jnp.bfloat16)] * (owners - NEAR),
        compiler_params=params(8),
        cost_estimate=pl.CostEstimate(
            flops=STEP_FLOPS, bytes_accessed=count * height * side, transcendentals=0
        ),
    )(lists, own, *parts, *after)


def near_kernel(slots, lists_ref, *refs):
    chunks, outs = refs[:-NEAR], refs[-NEAR:]
    row = lax.axis_index("row")
    start = 0
    for chunk in chunks:
        count, height, side = chunk.shape
        tiles = [chunk[t].astype(jnp.float32) for t in range(count)]
        for d, out in enumerate(outs):
            for k in range(slots):
                out[k, start : start + height] = listed_tile(lists_ref[(row ^ d) * slots + k, :1], tiles)
        start += height


def pick_near(lists, slots, chunks):
    side = sum(chunk.shape[1] for chunk in chunks)
    shape = jax.ShapeDtypeStruct((slots, side, chunks[0].shape[2]), jnp.bfloat16)
    return pl.pallas_call(
        functools.partial(near_kernel, slots),
        in_specs=[VMEM] * (1 + len(chunks)),
        out_specs=[VMEM] * NEAR,
        out_shape=[shape] * NEAR,
        compiler_params=params(8),
        cost_estimate=pl.CostEstimate(flops=STEP_FLOPS, bytes_accessed=side * side, transcendentals=0),
    )(lists, *chunks)


def contract_kernel(base, count, start, before_ref, row_phi_ref, col_phi_ref, *refs):
    gots, out = refs[:count], refs[-1]
    row = lax.axis_index("row")
    cut = pl.ds(start, gots[0].shape[1])
    density = before_ref[...]
    for d, got in enumerate(gots, base):
        slots = got.shape[0]
        for k in range(slots):
            m = (row ^ d) * slots + k
            half = jnp.dot(got[k], row_phi_ref[m], preferred_element_type=jnp.float32)
            density += jnp.sum(col_phi_ref[m, cut].astype(jnp.float32) * half, axis=0, keepdims=True)
    out[...] = density


def contract(before, row_phi, col_phi, gots, base, start, after=()):
    received, side, points = col_phi.shape
    slots, height, _ = gots[0].shape
    return pl.pallas_call(
        functools.partial(contract_kernel, base, len(gots), start),
        in_specs=[VMEM] * (3 + len(gots)) + [ANY] * len(after),
        out_specs=VMEM,
        out_shape=jax.ShapeDtypeStruct((1, points), jnp.float32),
        compiler_params=params(8),
        cost_estimate=pl.CostEstimate(
            flops=STEP_FLOPS,
            bytes_accessed=received * side * points,
            transcendentals=0,
        ),
    )(before, row_phi, col_phi, *gots, *after)


def swap(value, axis, d):
    return lax.ppermute(value, axis, [(i, i ^ d) for i in range(lax.axis_size(axis))])


def local(coeff_rows, coeff_cols, occupation, send_list, row_phi, col_phi):
    states, owners = lax.axis_size("state"), lax.axis_size("row")
    side, slots = coeff_rows.shape[0] // states, send_list.shape[-1]
    bounds = [side * sum(PARTS[:n]) // sum(PARTS) // 16 * 16 for n in range(len(PARTS) + 1)]
    heights = [after - before for before, after in zip(bounds, bounds[1:])]
    row_phi, col_phi, picks = row_phi[0, 0, 0], col_phi[0, 0, 0], send_list[0, 0, 0]
    factors = coeff_rows, occupation[None, :], coeff_cols.reshape(-1, side, coeff_cols.shape[1]), side

    lists = jnp.broadcast_to(picks.reshape(-1, 1, 1), (picks.size, 8, side))
    early = first(heights[0], *factors)
    parts = rest(heights, *factors, early)
    parts[0, 1] = early

    def send(c):
        return [swap(parts[c, d], "state", d) for d in range(1, states)]

    arrived = [send(c) for c in range(min(AHEAD, len(heights)))]
    starts = [sum(heights[:c]) for c in range(len(heights))]
    tiles, far, after = [], [], []
    density = jnp.zeros((1, row_phi.shape[-1]), jnp.float32)
    for c in range(len(heights)):
        chunk, *outgoing = pick(lists, slots, parts[c, 0], arrived[c], after)
        tiles.append(chunk)
        after = [chunk]
        far.append([swap(out, "row", d) for d, out in enumerate(outgoing, NEAR)])
        if c + AHEAD < len(heights):
            for d in range(1, states):
                parts[c + AHEAD, d], _ = lax.optimization_barrier((parts[c + AHEAD, d], chunk))
            arrived.append(send(c + AHEAD))
        if 1 <= c < len(heights) - 1:
            density = contract(density, row_phi, col_phi, far[c - 1], NEAR, starts[c - 1], after)
            after = [density]
    mine, other = pick_near(lists, slots, tiles)
    density = contract(density, row_phi, col_phi, far[-2], NEAR, starts[-2], [mine])
    density = contract(density, row_phi, col_phi, [mine, swap(other, "row", 1)], 0, 0)
    density = contract(density, row_phi, col_phi, far[-1], NEAR, starts[-1])
    return density.reshape(1, 1, 1, -1)


def solution(mesh):
    in_specs = (
        P("row", "state"),
        P("col", "state"),
        P("state"),
        P("state", "row", "col", None, None),
        P("state", "row", "col", None, None, None),
        P("state", "row", "col", None, None, None),
    )
    out_specs = P("state", "row", "col", None)
    return jax.shard_map(local, mesh=mesh, in_specs=in_specs, out_specs=out_specs, check_vma=False)
```
